256 devices in a mesh: space: 64 (over z, y, core), cfg: 4 (over x).
Axes of the slice: x: 4, y: 4, z: 8, core: 2. Of those that a mesh axis runs over, the one named last changes fastest.
Arguments:
- snapshots: bfloat16 [393216, 2048], P('space', 'cfg'), may hold values from -6 to 6
- sketch_input: bfloat16 [2048, 256], P('cfg'), may hold values from -0.125 to 0.125
Outputs:
- basis: float32 [393216, 256], P(('space', 'cfg'))
- coefficients: float32 [256, 2048], P('space', 'cfg')
The draws below stay inside these ranges and needn't reach their ends.
All inputs are finite; a program needn't handle non-finite values.
Results may differ from the reference program's by a relative error of at most 0.0055.
Values may be sent and summed in bfloat16 or wider, within the bound.
No kernel may reach another device: no remote copies, remote signals or barrier semaphores. Data moves between devices by JAX's collectives and lax.ppermute only.
A program may use at most 64 MiB of HBM per device.

```python
import jax
import jax.numpy as jnp
from jax import lax

COLS = 2048
RANK = 256
CHOL_BLOCK = 64
ROWS = 393216


def steps_of(stream_key, extent, shards, least, top_value):
    loudness = 1.0
    for position, parts in shards:
        draws = jax.random.uniform(jax.random.fold_in(jax.random.fold_in(stream_key, 6), position), (parts,), jnp.float32, least / len(shards), top_value / len(shards))
        loudness = loudness * jnp.repeat(jnp.exp(draws), extent[position] // parts).reshape((-1,) + (1,) * (len(extent) - 1 - position))
    return loudness


def noise(stream_key, shape, scale, limit, pieces=(), kind=jnp.bfloat16):
    values = scale * jax.random.normal(stream_key, shape, jnp.float32)
    if pieces:
        values = values * steps_of(stream_key, shape, pieces, -0.22, 0.18)
    return jnp.clip(values, -limit, limit).astype(kind)


def setup_inputs(seed: int = 0) -> dict:
    arg_keys = jax.random.split(jax.random.key(seed), 3)
    snapshots = noise(arg_keys[0], (ROWS, COLS), 1.0, 6.0, ((0, 64), (1, 4)))
    sketch_input = noise(arg_keys[1], (COLS, RANK), COLS ** -0.5, 0.125, ((0, 4),))
    return {"snapshots": snapshots, "sketch_input": sketch_input}


def blocked_cholesky(gram):
    order = gram.shape[0]
    lower = jnp.zeros_like(gram)
    rest = gram
    for first in range(0, order, CHOL_BLOCK):
        last = first + CHOL_BLOCK
        diag = jnp.linalg.cholesky(rest[first:last, first:last])
        lower = lower.at[first:last, first:last].set(diag)
        if last < order:
            below = rest[last:, first:last]
            solved = lax.linalg.triangular_solve(diag, below, left_side=False, lower=True, transpose_a=True)
            lower = lower.at[last:, first:last].set(solved)
            update = jnp.dot(solved, solved.T, precision=lax.Precision.HIGHEST)
            rest = rest.at[last:, last:].add(-update)
    return lower

def reference(snapshots, sketch_input):
    sketch = jnp.dot(snapshots.astype(jnp.float32), sketch_input.astype(jnp.float32), preferred_element_type=jnp.float32)
    gram = jnp.dot(sketch.T, sketch, precision=lax.Precision.HIGHEST)
    lower = blocked_cholesky(gram)
    ident = jnp.eye(RANK, dtype=jnp.float32)
    inverse = lax.linalg.triangular_solve(lower, ident, left_side=True, lower=True)
    ortho = jnp.dot(sketch, inverse.T, precision=lax.Precision.HIGHEST)
    basis = ortho * jnp.sqrt(jnp.float32(ROWS))
    sketch_low = sketch.astype(jnp.bfloat16)
    cross = lax.dot_general(sketch_low.astype(jnp.float32), snapshots.astype(jnp.float32), (((0,), (0,)), ((), ())), preferred_element_type=jnp.float32)
    coefficients = jnp.dot(inverse, cross, precision=lax.Precision.HIGHEST) * jnp.sqrt(jnp.float32(COLS) / jnp.float32(ROWS))
    return (basis, coefficients)
```

```python
import functools

import jax
import jax.numpy as jnp
from jax import lax
from jax.experimental import pallas as pl
from jax.experimental.pallas import tpu as pltpu
from jax.sharding import Mesh, PartitionSpec as P

HIGHEST = lax.Precision.HIGHEST
CHOL_BLOCK = 64
PIVOTS = 8
PAD = 16
VMEM_LIMIT = 48 * 1024 * 1024
FIRST = (((0,), (0,)), ((), ()))


def params():
    return pltpu.CompilerParams(vmem_limit_bytes=VMEM_LIMIT)


def partial_kernel(which, snap, omega, out):
    value = jnp.dot(snap[...], omega[...], preferred_element_type=jnp.float32)
    top = jnp.max(jnp.abs(value), axis=0, keepdims=True)
    power = jnp.ceil(jnp.log2(jnp.maximum(top, 1e-30))) + 1.0
    rows = value.shape[0]
    out[:rows, :] = value * jnp.exp2(14.0 - power)
    out[rows:, :] = jnp.broadcast_to(power, (PAD, power.shape[1]))


def partial_chunk(snapshots, omega, chunk, rows):
    cols, rank = omega.shape
    return pl.pallas_call(
        partial_kernel,
        grid_spec=pltpu.PrefetchScalarGridSpec(
            num_scalar_prefetch=1,
            grid=(1,),
            in_specs=[
                pl.BlockSpec((rows, cols), lambda i, which: (which[0], 0)),
                pl.BlockSpec((cols, rank), lambda i, which: (0, 0)),
            ],
            out_specs=pl.BlockSpec((rows + PAD, rank), lambda i, which: (0, 0)),
        ),
        out_shape=jax.ShapeDtypeStruct((rows + PAD, rank), jnp.float32),
        compiler_params=params(),
        name="partial_chunk",
    )(chunk, snapshots, omega)


def own_kernel(which, snap, omega, out):
    out[...] = jnp.dot(snap[...], omega[...], preferred_element_type=jnp.float32)


def own_chunk(snapshots, omega, chunk, rows):
    cols, rank = omega.shape
    return pl.pallas_call(
        own_kernel,
        grid_spec=pltpu.PrefetchScalarGridSpec(
            num_scalar_prefetch=1,
            grid=(1,),
            in_specs=[
                pl.BlockSpec((rows, cols), lambda i, which: (which[0], 0)),
                pl.BlockSpec((cols, rank), lambda i, which: (0, 0)),
            ],
            out_specs=pl.BlockSpec((rows, rank), lambda i, which: (0, 0)),
        ),
        out_shape=jax.ShapeDtypeStruct((rows, rank), jnp.float32),
        compiler_params=params(),
        name="own_chunk",
    )(chunk, snapshots, omega)


def gram_kernel(mine, out):
    rank = mine.shape[1]
    gram = lax.dot_general(mine[...], mine[...], FIRST, precision=HIGHEST)
    for h in range(rank // 128):
        out[h] = gram[:, 128 * h : 128 * (h + 1)].reshape(rank // 8, 8, 128)


def gram_tiles(mine):
    rank = mine.shape[1]
    tiles = pl.pallas_call(
        gram_kernel,
        out_shape=jax.ShapeDtypeStruct((rank // 128, rank // 8, 8, 128), jnp.float32),
        compiler_params=params(),
        name="gram_tiles",
    )(mine)
    return tiles.reshape(-1, 8, 128)


def cross_kernel(which, snap, *refs):
    lows, out = refs[:-1], refs[-1]
    step = pl.program_id(0)
    for i, low in enumerate(lows):

        @pl.when(step == i)
        def _():
            part = lax.dot_general(low[...], snap[...], FIRST, preferred_element_type=jnp.float32)
            if i == 0:
                out[...] = part
            else:
                out[...] += part


def cross_part(snapshots, order, lows):
    rows, rank = lows[0].shape
    cols = snapshots.shape[1]
    return pl.pallas_call(
        cross_kernel,
        grid_spec=pltpu.PrefetchScalarGridSpec(
            num_scalar_prefetch=1,
            grid=(len(lows),),
            in_specs=[pl.BlockSpec((rows, cols), lambda i, which: (which[i], 0))]
            + [pl.BlockSpec((rows, rank), lambda i, which: (0, 0))] * len(lows),
            out_specs=pl.BlockSpec((rank, cols), lambda i, which: (0, 0)),
        ),
        out_shape=jax.ShapeDtypeStruct((rank, cols), jnp.float32),
        compiler_params=params(),
        name="cross_part",
    )(order, snapshots, *lows)


def eliminate(groups, size, step):
    sub = lax.broadcasted_iota(jnp.int32, (8, 128), 0)
    count = size // 8
    for k in range(0, size, step):
        g, s = divmod(k, 8)
        cols = {
            i: [jnp.broadcast_to(groups[i][:, k + j : k + j + 1], (8, 128)) for j in range(step)]
            for i in range(g, count)
        }
        pivot = [
            [
                jnp.broadcast_to(cols[g][j][s + i : s + i + 1, :], (8, 128)) if j <= i else None
                for j in range(step)
            ]
            for i in range(step)
        ]
        inv, low = [], [[None] * step for _ in range(step)]
        for j in range(step):
            inv.append(1.0 / pivot[j][j])
            for i in range(j + 1, step):
                low[i][j] = pivot[i][j] * inv[j]
            for i in range(j + 1, step):
                for m in range(j + 1, i + 1):
                    pivot[i][m] = pivot[i][m] - low[i][j] * pivot[m][j]
        rows = []
        for i in range(step):
            row = jnp.broadcast_to(groups[g][s + i : s + i + 1, :], (8, 128))
            for j in range(i):
                row = row - low[i][j] * rows[j]
            rows.append(row)
        for i in range(g, count):
            new = groups[i]
            if i > g or s + step < 8:
                mult = []
                for j in range(step):
                    c = cols[i][j]
                    for q in range(j):
                        c = c - mult[q] * pivot[j][q]
                    mult.append(c * inv[j])
                for j in range(step):
                    new = new - mult[j] * rows[j]
            if i == g:
                for j in range(step):
                    new = jnp.where(sub == s + j, rows[j], new)
                if s:
                    new = jnp.where(sub < s, groups[g], new)
            groups[i] = new
    return groups


def block_inverse(block, step):
    size = block.shape[0]
    at = lambda d: lax.broadcasted_iota(jnp.int32, (size, size), d)
    eye = at(0) == at(1)
    both = jnp.concatenate([block, eye.astype(jnp.float32)], axis=1)
    groups = [both[8 * i : 8 * i + 8] for i in range(size // 8)]
    both = jnp.concatenate(eliminate(groups, size, step), axis=0)
    diag = jnp.sum(jnp.where(eye, both[:, :size], 0.0), axis=1, keepdims=True)
    return both[:, size:] * lax.rsqrt(diag)


def inverse_kernel(tiles, inverse, work, rest):
    n = work.shape[0]
    for h in range(n // 128):
        work[:, 128 * h : 128 * (h + 1)] = tiles[h].reshape(n, 128)
    inverse[...] = jnp.zeros_like(inverse)
    rest[...] = jnp.zeros_like(rest)
    for k in range(0, n, CHOL_BLOCK):
        e = k + CHOL_BLOCK
        w = block_inverse(work[k:e, k:e], PIVOTS)
        inverse[k:e, k:e] = w
        if k:
            inverse[k:e, :k] = jnp.dot(w, rest[k:e, :k], precision=HIGHEST)
        if e < n:
            solved = jnp.dot(w, work[k:e, e:], precision=HIGHEST)
            work[e:, e:] -= lax.dot_general(solved, solved, FIRST, precision=HIGHEST)
            rest[e:, :e] -= lax.dot_general(solved, inverse[k:e, :e], FIRST, precision=HIGHEST)


def lower_inverse(tiles, rank):
    return pl.pallas_call(
        inverse_kernel,
        out_shape=jax.ShapeDtypeStruct((rank, rank), jnp.float32),
        scratch_shapes=[pltpu.VMEM((rank, rank), jnp.float32)] * 2,
        compiler_params=params(),
        name="lower_inverse",
    )(tiles.reshape(rank // 128, rank // 8, 8, 128))


def coeff_kernel(inverse, cross, out, *, factor):
    value = jnp.dot(inverse[...], cross[...], precision=HIGHEST) * factor
    rank = value.shape[0]
    cores, chips, sub, _ = out.shape
    blocks = value.shape[1] // 128
    each = sub // blocks
    for q in range(blocks):
        part = value[:, 128 * q : 128 * (q + 1)].reshape(chips, cores * each, 128)
        for c in range(cores):
            out[c, :, each * q : each * (q + 1), :] = part[:, each * c : each * (c + 1), :]


def coeff_parts(inverse, cross, factor, cores, chips):
    rank, cols = cross.shape
    sub = rank // (cores * chips) * (cols // 128)
    return pl.pallas_call(
        functools.partial(coeff_kernel, factor=factor),
        out_shape=jax.ShapeDtypeStruct((cores, chips, sub, 128), jnp.float32),
        compiler_params=params(),
        name="coeff_parts",
    )(inverse, cross)


def basis_kernel(mine, inverse, out, *, factor):
    dims = (((1,), (1,)), ((), ()))
    out[...] = lax.dot_general(mine[...], inverse[...], dims, precision=HIGHEST) * factor


def basis_rows(mine, inverse, factor):
    rows, rank = mine.shape
    tile = rows // 4
    return pl.pallas_call(
        functools.partial(basis_kernel, factor=factor),
        grid=(rows // tile,),
        in_specs=[
            pl.BlockSpec((tile, rank), lambda i: (i, 0)),
            pl.BlockSpec((rank, rank), lambda i: (0, 0)),
        ],
        out_specs=pl.BlockSpec((tile, rank), lambda i: (i, 0)),
        out_shape=jax.ShapeDtypeStruct((rows, rank), jnp.float32),
        compiler_params=params(),
        name="basis_rows",
    )(mine, inverse)


def shift(value, axis, by):
    n = lax.axis_size(axis)
    return lax.ppermute(value, axis, [(i, (i + by) % n) for i in range(n)])


def per_device(snapshots, omega):
    x = lax.axis_index("x")
    nx, chips, cores = 4, lax.axis_size("z") * lax.axis_size("y"), lax.axis_size("c")
    space = ("z", "y", "c")
    rank = omega.shape[1]
    rows = snapshots.shape[0] // nx
    total_rows = snapshots.shape[0] * chips * cores
    total_cols = snapshots.shape[1] * nx
    at = lambda d: lax.rem(x + d, nx).astype(jnp.int32).reshape(1)

    mine = own_chunk(snapshots, omega, at(0), rows)
    for d in (2, 1, 3):
        sent = partial_chunk(snapshots, omega, at(d), rows).astype(jnp.float16)
        got = shift(sent, "x", d).astype(jnp.float32)
        mine = mine + got[:rows] * jnp.exp2(got[rows : rows + 1] - 14.0)
    low = mine.astype(jnp.bfloat16)

    half = rows // 2
    from_left = shift(low, "x", 1)
    from_right = shift(low, "x", -1)
    far = jnp.concatenate([shift(from_left[:half], "x", 1), shift(from_right[half:], "x", -1)], axis=0)
    order = jnp.concatenate([at(0), at(3), at(1), at(2)])
    cross = cross_part(snapshots, order, [low, from_left, from_right, far])

    tiles = gram_tiles(mine)
    tile = jnp.sum(lax.all_to_all(tiles, space, 0, 0, tiled=True), axis=0)
    tile = (tile + shift(tile, "x", 2)) + (shift(tile, "x", 1) + shift(tile, "x", 3))
    tiles = lax.all_to_all(jnp.broadcast_to(tile, tiles.shape), space, 0, 0, tiled=True)
    inverse = lower_inverse(tiles, rank)

    parts = coeff_parts(inverse, cross, (total_cols / total_rows) ** 0.5, cores, chips)
    c = lax.axis_index("c")
    keep = lax.dynamic_index_in_dim(parts, c, 0, keepdims=False)
    send = lax.dynamic_index_in_dim(parts, 1 - c, 0, keepdims=False)
    both = keep + shift(send, "c", 1)
    coeff = jnp.sum(lax.all_to_all(both, ("z", "y"), 0, 0, tiled=True), axis=0)
    blocks = snapshots.shape[1] // 128
    coeff = coeff.reshape(blocks, -1, 128).transpose(1, 0, 2).reshape(-1, snapshots.shape[1])

    basis = basis_rows(mine, inverse, total_rows**0.5)
    return basis, coeff


def solution(mesh):
    fine = Mesh(mesh.devices.reshape(8, 4, 2, 4), ("z", "y", "c", "x"))
    space = ("z", "y", "c")
    return jax.shard_map(
        per_device,
        mesh=fine,
        in_specs=(P(space, "x"), P("x", None)),
        out_specs=(P(space + ("x",), None), P(space, "x")),
        check_vma=False,
    )
```

```python
import functools

import jax
import jax.numpy as jnp
from jax import lax
from jax.experimental import pallas as pl
from jax.experimental.pallas import tpu as pltpu
from jax.sharding import Mesh, PartitionSpec as P

HIGHEST = lax.Precision.HIGHEST
CHOL_BLOCK = 64
PIVOTS = 8
PAD = 16
MIB = 1024 * 1024
FIRST = (((0,), (0,)), ((), ()))


def params(mib=16):
    return pltpu.CompilerParams(vmem_limit_bytes=mib * MIB)


def cost(flops, nbytes):
    return pl.CostEstimate(flops=flops, bytes_accessed=nbytes, transcendentals=0)


def sketch_kernel(which, snap, omega, out, *, scaled, pad):
    n, half, _ = out.shape
    half -= pad
    value = jnp.dot(snap[...], omega[...], preferred_element_type=jnp.float32)
    for h in range(n):
        part = value[half * h : half * (h + 1)]
        if pad:
            top = jnp.max(jnp.abs(part), axis=0, keepdims=True)
            power = jnp.ceil(jnp.log2(jnp.maximum(top, 1e-30))) + 1.0
            scale = jnp.exp2(14.0 - power)
            part = part * jnp.where(pl.program_id(0) * n + h < scaled, scale, 1.0)
            out[h, half:, :] = jnp.broadcast_to(power, (pad, power.shape[1]))
        out[h, :half, :] = part


def sketch_rows(snapshots, omega, which, half, per_step, scaled, pad, name):
    cols, rank = omega.shape
    n = which.shape[0]
    return pl.pallas_call(
        functools.partial(sketch_kernel, scaled=scaled, pad=pad),
        grid_spec=pltpu.PrefetchScalarGridSpec(
            num_scalar_prefetch=1,
            grid=(n,),
            in_specs=[
                pl.BlockSpec((per_step * half, cols), lambda i, which: (which[i], 0)),
                pl.BlockSpec((cols, rank), lambda i, which: (0, 0)),
            ],
            out_specs=pl.BlockSpec((per_step, half + pad, rank), lambda i, which: (i, 0, 0)),
        ),
        out_shape=jax.ShapeDtypeStruct((n * per_step, half + pad, rank), jnp.float32),
        compiler_params=params(48),
        cost_estimate=cost(2 * n * per_step * half * cols * rank, 4 * n * per_step * half * cols),
        name=name,
    )(which, snapshots, omega)


def add_back(got, half):
    power = got[half : half + 1].astype(jnp.float32)
    return got[:half].astype(jnp.float32) * jnp.exp2(power - 14.0)


def relay(got, later, half):
    before = got[half : half + 1].astype(jnp.float32)
    power = jnp.maximum(before, later[half : half + 1]) + 1.0
    value = got.astype(jnp.float32) * jnp.exp2(before - 14.0) + later
    value = value * jnp.exp2(14.0 - power)
    row = lax.broadcasted_iota(jnp.int32, value.shape, 0)
    return jnp.where(row < half, value, power).astype(jnp.float16)


def gram_kernel(top, bottom, out, low):
    half = top.shape[0]
    out[...] = lax.dot_general(top[...], top[...], FIRST, precision=HIGHEST) + lax.dot_general(
        bottom[...], bottom[...], FIRST, precision=HIGHEST
    )
    low[:half, :] = top[...].astype(low.dtype)
    low[half:, :] = bottom[...].astype(low.dtype)


def gram_of(top, bottom):
    rows, rank = top.shape
    return pl.pallas_call(
        gram_kernel,
        out_shape=[
            jax.ShapeDtypeStruct((rank, rank), jnp.float32),
            jax.ShapeDtypeStruct((2 * rows, rank), jnp.bfloat16),
        ],
        compiler_params=params(),
        cost_estimate=cost(24 * rows * rank * rank, 12 * rows * rank),
        name="gram_of",
    )(top, bottom)


def spread_kernel(got, out):
    total = got[0]
    for i in range(1, got.shape[0]):
        total = total + got[i]
    for i in range(out.shape[0]):
        out[i] = total


def sum_copies(got, n):
    return pl.pallas_call(
        spread_kernel,
        out_shape=jax.ShapeDtypeStruct((n,) + got.shape[1:], got.dtype),
        compiler_params=params(),
        name="sum_copies",
    )(got)


def cross_kernel(which, snap, *refs, has_before):
    refs, out = refs[:-1], refs[-1]
    before, lows = (refs[0], refs[1:]) if has_before else (None, refs)
    step = pl.program_id(0)
    for i, low in enumerate(lows):

        @pl.when(step == i)
        def _():
            part = lax.dot_general(low[...], snap[...], FIRST, preferred_element_type=jnp.float32)
            if i:
                out[...] += part
            elif before is not None:
                out[...] = before[...] + part
            else:
                out[...] = part


def cross_part(snapshots, order, lows, before=None):
    rows, rank = lows[0].shape
    cols = snapshots.shape[1]
    n = len(lows)
    whole = lambda i, which: (0, 0)
    start = [] if before is None else [before]
    return pl.pallas_call(
        functools.partial(cross_kernel, has_before=before is not None),
        grid_spec=pltpu.PrefetchScalarGridSpec(
            num_scalar_prefetch=1,
            grid=(n,),
            in_specs=[pl.BlockSpec((rows, cols), lambda i, which: (which[i], 0))]
            + [pl.BlockSpec((rank, cols), whole)] * len(start)
            + [pl.BlockSpec((rows, rank), whole)] * n,
            out_specs=pl.BlockSpec((rank, cols), whole),
        ),
        out_shape=jax.ShapeDtypeStruct((rank, cols), jnp.float32),
        compiler_params=params(48),
        cost_estimate=cost(2 * n * rows * cols * rank, 2 * n * rows * (cols + rank)),
        name="cross_part",
    )(order, snapshots, *start, *lows)


def eliminate(groups, size, step):
    sub = lax.broadcasted_iota(jnp.int32, (8, 128), 0)
    count = size // 8
    for k in range(0, size, step):
        g, s = divmod(k, 8)
        cols = {
            i: [jnp.broadcast_to(groups[i][:, k + j : k + j + 1], (8, 128)) for j in range(step)]
            for i in range(g, count)
        }
        pivot = [
            [
                jnp.broadcast_to(cols[g][j][s + i : s + i + 1, :], (8, 128)) if j <= i else None
                for j in range(step)
            ]
            for i in range(step)
        ]
        inv, low = [], [[None] * step for _ in range(step)]
        for j in range(step):
            if j % 2 == 0:
                a, b, d = pivot[j][j], pivot[j + 1][j], pivot[j + 1][j + 1]
                guess = a * (1.0 / (a * d - b * b))
                inv.append(1.0 / a)
            else:
                inv.append(guess * (2.0 - pivot[j][j] * guess))
            for i in range(j + 1, step):
                low[i][j] = pivot[i][j] * inv[j]
            for i in range(j + 1, step):
                for m in range(j + 1, i + 1):
                    pivot[i][m] = pivot[i][m] - low[i][j] * pivot[m][j]
        rows = []
        for i in range(step):
            row = jnp.broadcast_to(groups[g][s + i : s + i + 1, :], (8, 128))
            for j in range(i):
                row = row - low[i][j] * rows[j]
            rows.append(row)
        for i in range(g, count):
            new = groups[i]
            if i > g or s + step < 8:
                mult = []
                for j in range(step):
                    c = cols[i][j]
                    for q in range(j):
                        c = c - mult[q] * pivot[j][q]
                    mult.append(c * inv[j])
                for j in range(step):
                    new = new - mult[j] * rows[j]
            if i == g:
                for j in range(step):
                    new = jnp.where(sub == s + j, rows[j], new)
                if s:
                    new = jnp.where(sub < s, groups[g], new)
            groups[i] = new
    return groups


def block_inverse(block, step):
    size = block.shape[0]
    at = lambda d: lax.broadcasted_iota(jnp.int32, (size, size), d)
    eye = at(0) == at(1)
    both = jnp.concatenate([block, eye.astype(jnp.float32)], axis=1)
    groups = [both[8 * i : 8 * i + 8] for i in range(size // 8)]
    both = jnp.concatenate(eliminate(groups, size, step), axis=0)
    diag = jnp.sum(jnp.where(eye, both[:, :size], 0.0), axis=1, keepdims=True)
    return both[:, size:] * lax.rsqrt(diag)


def inverse_kernel(core, held, other, inverse, work, rest):
    n = work.shape[0]
    half = n // 2
    work[pl.ds(pl.multiple_of(core[0] * half, half), half), :] = held[...]
    work[pl.ds(pl.multiple_of((1 - core[0]) * half, half), half), :] = other[...]
    inverse[...] = jnp.zeros_like(inverse)
    rest[...] = jnp.zeros_like(rest)
    for k in range(0, n, CHOL_BLOCK):
        e = k + CHOL_BLOCK
        w = block_inverse(work[k:e, k:e], PIVOTS)
        inverse[k:e, k:e] = w
        if k:
            inverse[k:e, :k] = jnp.dot(w, rest[k:e, :k], precision=HIGHEST)
        if e < n:
            solved = jnp.dot(w, work[k:e, e:], precision=HIGHEST)
            work[e:, e:] -= lax.dot_general(solved, solved, FIRST, precision=HIGHEST)
            rest[e:, :e] -= lax.dot_general(solved, inverse[k:e, :e], FIRST, precision=HIGHEST)


def lower_inverse(core, held, other):
    half, rank = held.shape
    return pl.pallas_call(
        inverse_kernel,
        grid_spec=pltpu.PrefetchScalarGridSpec(
            num_scalar_prefetch=1,
            grid=(1,),
            in_specs=[pl.BlockSpec((half, rank), lambda i, core: (0, 0))] * 2,
            out_specs=pl.BlockSpec((rank, rank), lambda i, core: (0, 0)),
            scratch_shapes=[pltpu.VMEM((rank, rank), jnp.float32)] * 2,
        ),
        out_shape=jax.ShapeDtypeStruct((rank, rank), jnp.float32),
        compiler_params=params(),
        cost_estimate=cost(5 * 10**9, 4 * rank * rank),
        name="lower_inverse",
    )(core, held, other)


def coeff_kernel(which, inverse, near, low, snap, out, *, factor):
    cross = near[...] + lax.dot_general(
        low[...], snap[...], FIRST, preferred_element_type=jnp.float32
    )
    value = jnp.dot(inverse[...], cross, precision=HIGHEST) * factor
    cores, chips, sub, _ = out.shape
    blocks = value.shape[1] // 128
    each = sub // blocks
    for q in range(blocks):
        part = value[:, 128 * q : 128 * (q + 1)].reshape(chips, cores * each, 128)
        for c in range(cores):
            out[c, :, each * q : each * (q + 1), :] = part[:, each * c : each * (c + 1), :]


def coeff_parts(inverse, near, low, snapshots, block, factor, cores, chips):
    rank, cols = near.shape
    rows = low.shape[0]
    sub = rank // (cores * chips) * (cols // 128)
    whole = lambda *shape: pl.BlockSpec(shape, lambda i, which: (0,) * len(shape))
    return pl.pallas_call(
        functools.partial(coeff_kernel, factor=factor),
        grid_spec=pltpu.PrefetchScalarGridSpec(
            num_scalar_prefetch=1,
            grid=(1,),
            in_specs=[
                whole(rank, rank),
                whole(rank, cols),
                whole(rows, rank),
                pl.BlockSpec((rows, cols), lambda i, which: (which[0], 0)),
            ],
            out_specs=whole(cores, chips, sub, 128),
        ),
        out_shape=jax.ShapeDtypeStruct((cores, chips, sub, 128), jnp.float32),
        compiler_params=params(48),
        cost_estimate=cost(2 * rows * cols * rank + 12 * rank * rank * cols, 2 * rows * cols),
        name="coeff_parts",
    )(block, inverse, near, low, snapshots)


def basis_kernel(top, bottom, inverse, out, *, factor, steps):
    dims = (((1,), (1,)), ((), ()))
    mine = jnp.where(pl.program_id(0) < steps, top[...], bottom[...])
    out[...] = lax.dot_general(mine, inverse[...], dims, precision=HIGHEST) * factor


def basis_rows(top, bottom, inverse, factor):
    rows, rank = top.shape
    steps = 2
    tile = rows // steps
    return pl.pallas_call(
        functools.partial(basis_kernel, factor=factor, steps=steps),
        grid=(2 * steps,),
        in_specs=[
            pl.BlockSpec((tile, rank), lambda i: (jnp.minimum(i, steps - 1), 0)),
            pl.BlockSpec((tile, rank), lambda i: (jnp.maximum(i - steps, 0), 0)),
            pl.BlockSpec((rank, rank), lambda i: (0, 0)),
        ],
        out_specs=pl.BlockSpec((tile, rank), lambda i: (i, 0)),
        out_shape=jax.ShapeDtypeStruct((2 * rows, rank), jnp.float32),
        compiler_params=params(),
        cost_estimate=cost(24 * rows * rank * rank, 16 * rows * rank),
        name="basis_rows",
    )(top, bottom, inverse)


def shift(value, axis, by):
    n = lax.axis_size(axis)
    return lax.ppermute(value, axis, [(i, (i + by) % n) for i in range(n)])


def exchange(value, axes):
    return lax.all_to_all(value, axes, 0, 0, tiled=True)


def per_device(snapshots, omega):
    x, c = lax.axis_index("x"), lax.axis_index("c")
    nx, nz, cores = lax.axis_size("x"), lax.axis_size("z"), lax.axis_size("c")
    chips = nz * lax.axis_size("y")
    cols, rank = omega.shape
    rows = snapshots.shape[0] // nx
    half = rows // 2
    total_rows = snapshots.shape[0] * chips * cores
    total_cols = cols * nx
    ahead = lambda d: 2 * lax.rem(x + d, nx)
    at = lambda *places: jnp.stack(places).astype(jnp.int32)
    sketch = functools.partial(sketch_rows, snapshots, omega, half=half)
    half16 = lambda v: v.astype(jnp.float16)

    far = sketch(which=at(lax.rem(x + 2, nx)), per_step=2, scaled=2, pad=PAD, name="far_chunk")
    far_up, far_down = shift(half16(far[0]), "x", 1), shift(half16(far[1]), "x", -1)
    places = at(ahead(1) + 1, ahead(3), ahead(1), ahead(3) + 1)
    near = sketch(which=places, per_step=1, scaled=2, pad=PAD, name="near_chunks")
    near_up, near_down = shift(half16(near[0]), "x", 1), shift(half16(near[1]), "x", -1)
    own = sketch(which=at(x), per_step=2, scaled=0, pad=0, name="own_chunk")
    far_up = shift(relay(far_up, near[2], half), "x", 1)
    far_down = shift(relay(far_down, near[3], half), "x", -1)
    top = own[0] + add_back(near_down, half) + add_back(far_up, half)
    bottom = own[1] + add_back(near_up, half) + add_back(far_down, half)

    tie = lax.optimization_barrier
    block = lambda *ds: at(*[lax.rem(x + d, nx) for d in ds])
    gram, low = gram_of(top, bottom)
    halves = gram.reshape(cores, rank // cores, rank)
    pick = lambda v, i: lax.dynamic_index_in_dim(v, i, 0, keepdims=False)
    held = pick(halves, c) + shift(pick(halves, 1 - c), "c", 1)
    held, low = tie((held, low))
    left, right = shift(low, "x", 1), shift(low, "x", -1)
    cross = cross_part(snapshots, block(0), [low])
    held, cross = tie((exchange(held.reshape(nz, -1, rank), "z"), cross))

    held = exchange(sum_copies(held, lax.axis_size("y") * nx), ("y", "x"))

    held, low, cross = tie((sum_copies(held, nz), low, cross))
    across = shift(low, "x", 2)
    cross = cross_part(snapshots, block(3, 1), [left, right], cross)
    held, cross = tie((exchange(held, "z").reshape(-1, rank), cross))
    other = shift(held, "c", 1)
    inverse = lower_inverse(c.astype(jnp.int32).reshape(1), held, other)

    factor = (total_cols / total_rows) ** 0.5
    parts = coeff_parts(inverse, cross, across, snapshots, block(2), factor, cores, chips)
    both = pick(parts, c) + shift(pick(parts, 1 - c), "c", 1)
    coeff = jnp.sum(exchange(both, ("z", "y")), axis=0)
    coeff = coeff.reshape(cols // 128, -1, 128).transpose(1, 0, 2).reshape(-1, cols)

    basis = basis_rows(top, bottom, inverse, total_rows**0.5)
    return basis, coeff


def solution(mesh):
    fine = Mesh(mesh.devices.reshape(8, 4, 2, 4), ("z", "y", "c", "x"))
    space = ("z", "y", "c")
    return jax.shard_map(
        per_device,
        mesh=fine,
        in_specs=(P(space, "x"), P("x", None)),
        out_specs=(P(space + ("x",), None), P(space, "x")),
        check_vma=False,
    )
```

```python
import functools

import jax
import jax.numpy as jnp
from jax import lax
from jax.experimental import pallas as pl
from jax.experimental.pallas import tpu as pltpu
from jax.sharding import Mesh, PartitionSpec as P

HIGHEST = lax.Precision.HIGHEST
PAD = 16
MIB = 1024 * 1024
FIRST = (((0,), (0,)), ((), ()))


def params(mib=16):
    return pltpu.CompilerParams(vmem_limit_bytes=mib * MIB)


def cost(flops, nbytes):
    return pl.CostEstimate(flops=flops, bytes_accessed=nbytes, transcendentals=0)


def sketch_kernel(which, snap, omega, out, *, scaled, pad):
    n, half, _ = out.shape
    half -= pad
    value = jnp.dot(snap[...], omega[...], preferred_element_type=jnp.float32)
    for h in range(n):
        part = value[half * h : half * (h + 1)]
        if pad:
            top = jnp.max(jnp.abs(part), axis=0, keepdims=True)
            power = jnp.ceil(jnp.log2(jnp.maximum(top, 1e-30))) + 1.0
            scale = jnp.exp2(14.0 - power)
            part = part * jnp.where(pl.program_id(0) * n + h < scaled, scale, 1.0)
            out[h, half:, :] = jnp.broadcast_to(power, (pad, power.shape[1]))
        out[h, :half, :] = part


def sketch_rows(snapshots, omega, which, half, per_step, scaled, pad, name):
    cols, rank = omega.shape
    n = which.shape[0]
    return pl.pallas_call(
        functools.partial(sketch_kernel, scaled=scaled, pad=pad),
        grid_spec=pltpu.PrefetchScalarGridSpec(
            num_scalar_prefetch=1,
            grid=(n,),
            in_specs=[
                pl.BlockSpec((per_step * half, cols), lambda i, which: (which[i], 0)),
                pl.BlockSpec((cols, rank), lambda i, which: (0, 0)),
            ],
            out_specs=pl.BlockSpec((per_step, half + pad, rank), lambda i, which: (i, 0, 0)),
        ),
        out_shape=jax.ShapeDtypeStruct((n * per_step, half + pad, rank), jnp.float32),
        compiler_params=params(48),
        cost_estimate=cost(2 * n * per_step * half * cols * rank, 4 * n * per_step * half * cols),
        name=name,
    )(which, snapshots, omega)


def add_back(got, half):
    power = got[half : half + 1].astype(jnp.float32)
    return got[:half].astype(jnp.float32) * jnp.exp2(power - 14.0)


def relay(got, later, half):
    before = got[half : half + 1].astype(jnp.float32)
    power = jnp.maximum(before, later[half : half + 1]) + 1.0
    value = got.astype(jnp.float32) * jnp.exp2(before - 14.0) + later
    value = value * jnp.exp2(14.0 - power)
    row = lax.broadcasted_iota(jnp.int32, value.shape, 0)
    return jnp.where(row < half, value, power).astype(jnp.float16)


def gram_kernel(core, top, bottom, keep, send, low, buf):
    half, rows, rank = top.shape[0], keep.shape[0], top.shape[1]
    gram = lax.dot_general(top[...], top[...], FIRST, precision=HIGHEST) + lax.dot_general(
        bottom[...], bottom[...], FIRST, precision=HIGHEST
    )
    buf[:, :rank] = gram[: rank // 2]
    buf[:, rank:] = gram[rank // 2 :, rank // 2 :]
    keep[...] = buf[pl.ds(pl.multiple_of(core[0] * rows, rows), rows), :]
    send[...] = buf[pl.ds(pl.multiple_of((1 - core[0]) * rows, rows), rows), :]
    low[:half, :] = top[...].astype(low.dtype)
    low[half:, :] = bottom[...].astype(low.dtype)


def gram_of(core, top, bottom):
    rows, rank = top.shape
    vmem = pl.BlockSpec(memory_space=pltpu.VMEM)
    packed = (rank // 2, rank + rank // 2)
    return pl.pallas_call(
        gram_kernel,
        in_specs=[pl.BlockSpec(memory_space=pltpu.SMEM), vmem, vmem],
        out_specs=[vmem] * 3,
        out_shape=[jax.ShapeDtypeStruct((packed[0] // 2, packed[1]), jnp.float32)] * 2
        + [jax.ShapeDtypeStruct((2 * rows, rank), jnp.bfloat16)],
        scratch_shapes=[pltpu.VMEM(packed, jnp.float32)],
        compiler_params=params(),
        cost_estimate=cost(24 * rows * rank * rank, 12 * rows * rank),
        name="gram_of",
    )(core, top, bottom)


def spread_kernel(got, out):
    total = got[0]
    for i in range(1, got.shape[0]):
        total = total + got[i]
    for i in range(out.shape[0]):
        out[i] = total


def sum_copies(got, n):
    return pl.pallas_call(
        spread_kernel,
        out_shape=jax.ShapeDtypeStruct((n,) + got.shape[1:], got.dtype),
        compiler_params=params(),
        name="sum_copies",
    )(got)


def cross_kernel(which, snap, *refs, has_before):
    refs, out = refs[:-1], refs[-1]
    before, lows = (refs[0], refs[1:]) if has_before else (None, refs)
    step = pl.program_id(0)
    for i, low in enumerate(lows):

        @pl.when(step == i)
        def _():
            part = lax.dot_general(low[...], snap[...], FIRST, preferred_element_type=jnp.float32)
            if i:
                out[...] += part
            elif before is not None:
                out[...] = before[...] + part
            else:
                out[...] = part


def cross_part(snapshots, order, lows, before=None):
    rows, rank = lows[0].shape
    cols = snapshots.shape[1]
    n = len(lows)
    whole = lambda i, which: (0, 0)
    start = [] if before is None else [before]
    return pl.pallas_call(
        functools.partial(cross_kernel, has_before=before is not None),
        grid_spec=pltpu.PrefetchScalarGridSpec(
            num_scalar_prefetch=1,
            grid=(n,),
            in_specs=[pl.BlockSpec((rows, cols), lambda i, which: (which[i], 0))]
            + [pl.BlockSpec((rank, cols), whole)] * len(start)
            + [pl.BlockSpec((rows, rank), whole)] * n,
            out_specs=pl.BlockSpec((rank, cols), whole),
        ),
        out_shape=jax.ShapeDtypeStruct((rank, cols), jnp.float32),
        compiler_params=params(48),
        cost_estimate=cost(2 * n * rows * cols * rank, 2 * n * rows * (cols + rank)),
        name="cross_part",
    )(order, snapshots, *start, *lows)


def eliminate(groups, buf):
    shape = groups[0].shape
    sub = lax.broadcasted_iota(jnp.int32, shape, 0)
    lane = lax.broadcasted_iota(jnp.int32, shape, 1)
    spread = lambda v: jnp.broadcast_to(v, shape)
    diags = []
    for g in range(len(groups)):
        k = 8 * g
        cols = {
            i: [spread(groups[i][:, k + j : k + j + 1]) for j in range(8)]
            for i in range(g, len(groups))
        }
        base = g % 2 * 64
        for j in range(8):
            buf[base + 8 * j : base + 8 * j + 8, :] = cols[g][j]
        at = lambda i, j: base + 8 * j + i
        pivot = [[spread(buf[at(i, j) : at(i, j) + 1, :]) for j in range(i + 1)] for i in range(8)]
        inside = (lane >= k) & (lane < k + 8)
        here = jnp.where(inside, jnp.where(lane - k == sub, 1.0, 0.0), groups[g])
        inv, low = [], [[None] * 8 for _ in range(8)]
        for j in range(8):
            if j % 2 == 0:
                a, b, d = pivot[j][j], pivot[j + 1][j], pivot[j + 1][j + 1]
                guess = a * (1.0 / (a * d - b * b))
                inv.append(1.0 / a)
            else:
                inv.append(guess * (2.0 - pivot[j][j] * guess))
            for i in range(j + 1, 8):
                low[i][j] = pivot[i][j] * inv[j]
            for i in range(j + 1, 8):
                for m in range(j + 1, i + 1):
                    pivot[i][m] = pivot[i][m] - low[i][j] * pivot[m][j]
        rows = []
        for i in range(8):
            row = spread(here[i : i + 1, :])
            for j in range(i):
                row = row - low[i][j] * rows[j]
            rows.append(row)
        new, diag = rows[0], pivot[0][0]
        for j in range(1, 8):
            new = jnp.where(sub == j, rows[j], new)
            diag = jnp.where(sub == j, pivot[j][j], diag)
        groups[g] = new
        diags.append(diag)
        for i in range(g + 1, len(groups)):
            mult = []
            for j in range(8):
                c = cols[i][j]
                for q in range(j):
                    c = c - mult[q] * pivot[j][q]
                mult.append(c * inv[j])
            new = jnp.where(inside, 0.0, groups[i])
            for j in range(8):
                new = new - mult[j] * rows[j]
            groups[i] = new
    return [
        jnp.where(lane <= sub + 8 * g, v, 0.0) * lax.rsqrt(d)
        for g, (v, d) in enumerate(zip(groups, diags))
    ]


def block_inverse(block, buf):
    groups = [block[8 * i : 8 * i + 8] for i in range(block.shape[0] // 8)]
    return jnp.concatenate(eliminate(groups, buf), axis=0)


def inverse_kernel(core, held, other, inverse, packed, buf):
    rows, n = held.shape[0], inverse.shape[0] // 2
    packed[pl.ds(pl.multiple_of(core[0] * rows, rows), rows), :] = held[...]
    packed[pl.ds(pl.multiple_of((1 - core[0]) * rows, rows), rows), :] = other[...]
    first = block_inverse(packed[:, :n], buf)
    solved = jnp.dot(first, packed[:, n : 2 * n], precision=HIGHEST)
    inverse[:n, :n] = first
    inverse[:n, n:] = jnp.zeros((n, n), jnp.float32)
    update = lax.dot_general(solved, solved, FIRST, precision=HIGHEST)
    second = block_inverse(packed[:, 2 * n :] - update, buf)
    inverse[n:, n:] = second
    below = lax.dot_general(solved, first, FIRST, precision=HIGHEST)
    inverse[n:, :n] = -jnp.dot(second, below, precision=HIGHEST)


def lower_inverse(core, held, other):
    rows, width = held.shape
    n = width // 3
    vmem = pl.BlockSpec(memory_space=pltpu.VMEM)
    return pl.pallas_call(
        inverse_kernel,
        in_specs=[pl.BlockSpec(memory_space=pltpu.SMEM), vmem, vmem],
        out_specs=vmem,
        out_shape=jax.ShapeDtypeStruct((2 * n, 2 * n), jnp.float32),
        scratch_shapes=[
            pltpu.VMEM((2 * rows, width), jnp.float32),
            pltpu.VMEM((128, n), jnp.float32),
        ],
        compiler_params=params(),
        cost_estimate=cost(5 * 10**9, 4 * rows * width),
        name="lower_inverse",
    )(core, held, other)


def coeff_kernel(core, inverse, near, low, snap, keep, send, *, factor):
    cross = near[...] + lax.dot_general(
        low[...], snap[...], FIRST, preferred_element_type=jnp.float32
    )
    value = jnp.dot(inverse[...], cross, precision=HIGHEST) * factor
    chips, sub, _ = keep.shape
    blocks = value.shape[1] // 128
    each = sub // blocks
    first = core[0] == 0
    for q in range(blocks):
        part = value[:, 128 * q : 128 * (q + 1)].reshape(chips, 2 * each, 128)
        one, two = part[:, :each, :], part[:, each:, :]
        keep[:, each * q : each * (q + 1), :] = jnp.where(first, one, two)
        send[:, each * q : each * (q + 1), :] = jnp.where(first, two, one)


def coeff_parts(core_block, inverse, near, low, snapshots, factor, chips):
    rank, cols = near.shape
    rows = low.shape[0]
    sub = rank // (2 * chips) * (cols // 128)
    whole = lambda *shape: pl.BlockSpec(shape, lambda i, which: (0,) * len(shape))
    return pl.pallas_call(
        functools.partial(coeff_kernel, factor=factor),
        grid_spec=pltpu.PrefetchScalarGridSpec(
            num_scalar_prefetch=1,
            grid=(1,),
            in_specs=[
                whole(rank, rank),
                whole(rank, cols),
                whole(rows, rank),
                pl.BlockSpec((rows, cols), lambda i, which: (which[1], 0)),
            ],
            out_specs=[whole(chips, sub, 128)] * 2,
        ),
        out_shape=[jax.ShapeDtypeStruct((chips, sub, 128), jnp.float32)] * 2,
        compiler_params=params(48),
        cost_estimate=cost(2 * rows * cols * rank + 12 * rank * rank * cols, 2 * rows * cols),
        name="coeff_parts",
    )(core_block, inverse, near, low, snapshots)


def basis_kernel(top, bottom, inverse, out, *, factor, steps):
    dims = (((1,), (1,)), ((), ()))
    mine = jnp.where(pl.program_id(0) < steps, top[...], bottom[...])
    out[...] = lax.dot_general(mine, inverse[...], dims, precision=HIGHEST) * factor


def basis_rows(top, bottom, inverse, factor):
    rows, rank = top.shape
    steps = 2
    tile = rows // steps
    return pl.pallas_call(
        functools.partial(basis_kernel, factor=factor, steps=steps),
        grid=(2 * steps,),
        in_specs=[
            pl.BlockSpec((tile, rank), lambda i: (jnp.minimum(i, steps - 1), 0)),
            pl.BlockSpec((tile, rank), lambda i: (jnp.maximum(i - steps, 0), 0)),
            pl.BlockSpec((rank, rank), lambda i: (0, 0)),
        ],
        out_specs=pl.BlockSpec((tile, rank), lambda i: (i, 0)),
        out_shape=jax.ShapeDtypeStruct((2 * rows, rank), jnp.float32),
        compiler_params=params(),
        cost_estimate=cost(24 * rows * rank * rank, 16 * rows * rank),
        name="basis_rows",
    )(top, bottom, inverse)


def shift(value, axis, by):
    n = lax.axis_size(axis)
    return lax.ppermute(value, axis, [(i, (i + by) % n) for i in range(n)])


def exchange(value, axes):
    return lax.all_to_all(value, axes, 0, 0, tiled=True)


def per_device(snapshots, omega):
    x, c = lax.axis_index("x"), lax.axis_index("c")
    nx, nz, cores = lax.axis_size("x"), lax.axis_size("z"), lax.axis_size("c")
    chips = nz * lax.axis_size("y")
    cols, rank = omega.shape
    rows = snapshots.shape[0] // nx
    half = rows // 2
    total_rows = snapshots.shape[0] * chips * cores
    total_cols = cols * nx
    ahead = lambda d: 2 * lax.rem(x + d, nx)
    at = lambda *places: jnp.stack(places).astype(jnp.int32)
    sketch = functools.partial(sketch_rows, snapshots, omega, half=half)
    half16 = lambda v: v.astype(jnp.float16)

    far = sketch(which=at(lax.rem(x + 2, nx)), per_step=2, scaled=2, pad=PAD, name="far_chunk")
    far_up, far_down = shift(half16(far[0]), "x", 1), shift(half16(far[1]), "x", -1)
    places = at(ahead(1) + 1, ahead(3), ahead(1), ahead(3) + 1)
    near = sketch(which=places, per_step=1, scaled=2, pad=PAD, name="near_chunks")
    near_up, near_down = shift(half16(near[0]), "x", 1), shift(half16(near[1]), "x", -1)
    own = sketch(which=at(x), per_step=2, scaled=0, pad=0, name="own_chunk")
    far_up = shift(relay(far_up, near[2], half), "x", 1)
    far_down = shift(relay(far_down, near[3], half), "x", -1)
    top = own[0] + add_back(near_down, half) + add_back(far_up, half)
    bottom = own[1] + add_back(near_up, half) + add_back(far_down, half)

    tie = lax.optimization_barrier
    block = lambda *ds: at(*[lax.rem(x + d, nx) for d in ds])
    core = c.astype(jnp.int32).reshape(1)
    keep, send, low = gram_of(core, top, bottom)
    held = keep + shift(send, "c", 1)
    left, right = shift(low, "x", 1), shift(low, "x", -1)
    cross = cross_part(snapshots, block(0), [low])
    held, cross = tie((exchange(held.reshape(nz, -1, held.shape[1]), "z"), cross))

    held, cross = tie((sum_copies(held, lax.axis_size("y") * nx), cross))
    cross = cross_part(snapshots, block(3, 1), [left, right], cross)
    held, cross = tie((exchange(held, ("y", "x")), cross))

    low, cross = tie((low, cross))
    across = shift(low, "x", 2)
    held = exchange(sum_copies(held, nz), "z")
    held = held.reshape(-1, held.shape[2])
    other = shift(held, "c", 1)
    inverse = lower_inverse(core, held, other)

    factor = (total_cols / total_rows) ** 0.5
    where = at(c, lax.rem(x + 2, nx))
    keep, send = coeff_parts(where, inverse, cross, across, snapshots, factor, chips)
    both = keep + shift(send, "c", 1)
    coeff = jnp.sum(exchange(both, ("z", "y")), axis=0)
    coeff = coeff.reshape(cols // 128, -1, 128).transpose(1, 0, 2).reshape(-1, cols)

    basis = basis_rows(top, bottom, inverse, total_rows**0.5)
    return basis, coeff


def solution(mesh):
    fine = Mesh(mesh.devices.reshape(8, 4, 2, 4), ("z", "y", "c", "x"))
    space = ("z", "y", "c")
    return jax.shard_map(
        per_device,
        mesh=fine,
        in_specs=(P(space, "x"), P("x", None)),
        out_specs=(P(space + ("x",), None), P(space, "x")),
        check_vma=False,
    )
```

```python
import functools

import jax
import jax.numpy as jnp
from jax import lax
from jax.experimental import pallas as pl
from jax.experimental.pallas import tpu as pltpu
from jax.sharding import Mesh, PartitionSpec as P

HIGHEST = lax.Precision.HIGHEST
PAD = 16
MIB = 1024 * 1024
FIRST = (((0,), (0,)), ((), ()))


def params(mib=16):
    return pltpu.CompilerParams(vmem_limit_bytes=mib * MIB)


def cost(flops, nbytes):
    return pl.CostEstimate(flops=flops, bytes_accessed=nbytes, transcendentals=0)


def sketch_kernel(which, snap, omega, out, *, scaled, pad):
    n, half, _ = out.shape
    half -= pad
    value = jnp.dot(snap[...], omega[...], preferred_element_type=jnp.float32)
    for h in range(n):
        part = value[half * h : half * (h + 1)]
        if pad:
            top = jnp.max(jnp.abs(part), axis=0, keepdims=True)
            power = jnp.ceil(jnp.log2(jnp.maximum(top, 1e-30))) + 1.0
            scale = jnp.exp2(14.0 - power)
            part = part * jnp.where(pl.program_id(0) * n + h < scaled, scale, 1.0)
            out[h, half:, :] = jnp.broadcast_to(power, (pad, power.shape[1]))
        out[h, :half, :] = part


def sketch_rows(snapshots, omega, which, half, per_step, scaled, pad, name):
    cols, rank = omega.shape
    n = which.shape[0]
    return pl.pallas_call(
        functools.partial(sketch_kernel, scaled=scaled, pad=pad),
        grid_spec=pltpu.PrefetchScalarGridSpec(
            num_scalar_prefetch=1,
            grid=(n,),
            in_specs=[
                pl.BlockSpec((per_step * half, cols), lambda i, which: (which[i], 0)),
                pl.BlockSpec((cols, rank), lambda i, which: (0, 0)),
            ],
            out_specs=pl.BlockSpec((per_step, half + pad, rank), lambda i, which: (i, 0, 0)),
        ),
        out_shape=jax.ShapeDtypeStruct((n * per_step, half + pad, rank), jnp.float32),
        compiler_params=params(52),
        cost_estimate=cost(2 * n * per_step * half * cols * rank, 4 * n * per_step * half * cols),
        name=name,
    )(which, snapshots, omega)


def add_back(got, half):
    power = got[half : half + 1].astype(jnp.float32)
    return got[:half].astype(jnp.float32) * jnp.exp2(power - 14.0)


def relay(got, later, half):
    before = got[half : half + 1].astype(jnp.float32)
    power = jnp.maximum(before, later[half : half + 1]) + 1.0
    value = got.astype(jnp.float32) * jnp.exp2(before - 14.0) + later
    value = value * jnp.exp2(14.0 - power)
    row = lax.broadcasted_iota(jnp.int32, value.shape, 0)
    return jnp.where(row < half, value, power).astype(jnp.float16)


def gram_kernel(core, top, bottom, keep, send, low, buf):
    half, rows, rank = top.shape[0], keep.shape[0], top.shape[1]
    gram = lax.dot_general(top[...], top[...], FIRST, precision=HIGHEST) + lax.dot_general(
        bottom[...], bottom[...], FIRST, precision=HIGHEST
    )
    buf[:, :rank] = gram[: rank // 2]
    buf[:, rank:] = gram[rank // 2 :, rank // 2 :]
    keep[...] = buf[pl.ds(pl.multiple_of(core[0] * rows, rows), rows), :]
    send[...] = buf[pl.ds(pl.multiple_of((1 - core[0]) * rows, rows), rows), :]
    low[:half, :] = top[...].astype(low.dtype)
    low[half:, :] = bottom[...].astype(low.dtype)


def gram_of(core, top, bottom):
    rows, rank = top.shape
    vmem = pl.BlockSpec(memory_space=pltpu.VMEM)
    packed = (rank // 2, rank + rank // 2)
    return pl.pallas_call(
        gram_kernel,
        in_specs=[pl.BlockSpec(memory_space=pltpu.SMEM), vmem, vmem],
        out_specs=[vmem] * 3,
        out_shape=[jax.ShapeDtypeStruct((packed[0] // 2, packed[1]), jnp.float32)] * 2
        + [jax.ShapeDtypeStruct((2 * rows, rank), jnp.bfloat16)],
        scratch_shapes=[pltpu.VMEM(packed, jnp.float32)],
        compiler_params=params(),
        cost_estimate=cost(24 * rows * rank * rank, 12 * rows * rank),
        name="gram_of",
    )(core, top, bottom)


def spread_kernel(got, out):
    total = got[0]
    for i in range(1, got.shape[0]):
        total = total + got[i]
    for i in range(out.shape[0]):
        out[i] = total


def sum_copies(got, n):
    return pl.pallas_call(
        spread_kernel,
        out_shape=jax.ShapeDtypeStruct((n,) + got.shape[1:], got.dtype),
        compiler_params=params(),
        name="sum_copies",
    )(got)


def cross_kernel(which, snap, *refs, has_before):
    refs, out = refs[:-1], refs[-1]
    before, lows = (refs[0], refs[1:]) if has_before else (None, refs)
    step = pl.program_id(0)
    for i, low in enumerate(lows):

        @pl.when(step == i)
        def _():
            part = lax.dot_general(low[...], snap[...], FIRST, preferred_element_type=jnp.float32)
            if i:
                out[...] += part
            elif before is not None:
                out[...] = before[...] + part
            else:
                out[...] = part


def cross_part(snapshots, order, lows, before=None):
    rows, rank = lows[0].shape
    cols = snapshots.shape[1]
    n = len(lows)
    whole = lambda i, which: (0, 0)
    start = [] if before is None else [before]
    return pl.pallas_call(
        functools.partial(cross_kernel, has_before=before is not None),
        grid_spec=pltpu.PrefetchScalarGridSpec(
            num_scalar_prefetch=1,
            grid=(n,),
            in_specs=[pl.BlockSpec((rows, cols), lambda i, which: (which[i], 0))]
            + [pl.BlockSpec((rank, cols), whole)] * len(start)
            + [pl.BlockSpec((rows, rank), whole)] * n,
            out_specs=pl.BlockSpec((rank, cols), whole),
        ),
        out_shape=jax.ShapeDtypeStruct((rank, cols), jnp.float32),
        compiler_params=params(52),
        cost_estimate=cost(2 * n * rows * cols * rank, 2 * n * rows * (cols + rank)),
        name="cross_part",
    )(order, snapshots, *start, *lows)


def eliminate(groups, buf):
    shape = groups[0].shape
    sub = lax.broadcasted_iota(jnp.int32, shape, 0)
    lane = lax.broadcasted_iota(jnp.int32, shape, 1)
    spread = lambda v: jnp.broadcast_to(v, shape)
    diags = []
    for g in range(len(groups)):
        k = 8 * g
        cols = {
            i: [spread(groups[i][:, k + j : k + j + 1]) for j in range(8)]
            for i in range(g, len(groups))
        }
        base = g % 2 * 64
        for j in range(8):
            buf[base + 8 * j : base + 8 * j + 8, :] = cols[g][j]
        at = lambda i, j: base + 8 * j + i
        pivot = [[spread(buf[at(i, j) : at(i, j) + 1, :]) for j in range(i + 1)] for i in range(8)]
        inside = (lane >= k) & (lane < k + 8)
        here = jnp.where(inside, jnp.where(lane - k == sub, 1.0, 0.0), groups[g])
        inv, low = [], [[None] * 8 for _ in range(8)]
        for j in range(8):
            if j % 2 == 0:
                a, b, d = pivot[j][j], pivot[j + 1][j], pivot[j + 1][j + 1]
                guess = a * (1.0 / (a * d - b * b))
                inv.append(1.0 / a)
            else:
                inv.append(guess * (2.0 - pivot[j][j] * guess))
            for i in range(j + 1, 8):
                low[i][j] = pivot[i][j] * inv[j]
            for i in range(j + 1, 8):
                for m in range(j + 1, i + 1):
                    pivot[i][m] = pivot[i][m] - low[i][j] * pivot[m][j]
        rows = []
        for i in range(8):
            row = spread(here[i : i + 1, :])
            for j in range(i):
                row = row - low[i][j] * rows[j]
            rows.append(row)
        new, diag = rows[0], pivot[0][0]
        for j in range(1, 8):
            new = jnp.where(sub == j, rows[j], new)
            diag = jnp.where(sub == j, pivot[j][j], diag)
        groups[g] = new
        diags.append(diag)
        for i in range(g + 1, len(groups)):
            mult = []
            for j in range(8):
                c = cols[i][j]
                for q in range(j):
                    c = c - mult[q] * pivot[j][q]
                mult.append(c * inv[j])
            new = jnp.where(inside, 0.0, groups[i])
            for j in range(8):
                new = new - mult[j] * rows[j]
            groups[i] = new
    return [
        jnp.where(lane <= sub + 8 * g, v, 0.0) * lax.rsqrt(d)
        for g, (v, d) in enumerate(zip(groups, diags))
    ]


def block_inverse(block, buf):
    groups = [block[8 * i : 8 * i + 8] for i in range(block.shape[0] // 8)]
    return jnp.concatenate(eliminate(groups, buf), axis=0)


def inverse_kernel(core, held, other, inverse, packed, buf):
    rows, n = held.shape[0], inverse.shape[0] // 2
    packed[pl.ds(pl.multiple_of(core[0] * rows, rows), rows), :] = held[...]
    packed[pl.ds(pl.multiple_of((1 - core[0]) * rows, rows), rows), :] = other[...]
    first = block_inverse(packed[:, :n], buf)
    solved = jnp.dot(first, packed[:, n : 2 * n], precision=HIGHEST)
    inverse[:n, :n] = first
    inverse[:n, n:] = jnp.zeros((n, n), jnp.float32)
    update = lax.dot_general(solved, solved, FIRST, precision=HIGHEST)
    second = block_inverse(packed[:, 2 * n :] - update, buf)
    inverse[n:, n:] = second
    below = lax.dot_general(solved, first, FIRST, precision=HIGHEST)
    inverse[n:, :n] = -jnp.dot(second, below, precision=HIGHEST)


def lower_inverse(core, held, other):
    rows, width = held.shape
    n = width // 3
    vmem = pl.BlockSpec(memory_space=pltpu.VMEM)
    return pl.pallas_call(
        inverse_kernel,
        in_specs=[pl.BlockSpec(memory_space=pltpu.SMEM), vmem, vmem],
        out_specs=vmem,
        out_shape=jax.ShapeDtypeStruct((2 * n, 2 * n), jnp.float32),
        scratch_shapes=[
            pltpu.VMEM((2 * rows, width), jnp.float32),
            pltpu.VMEM((128, n), jnp.float32),
        ],
        compiler_params=params(),
        cost_estimate=cost(5 * 10**9, 4 * rows * width),
        name="lower_inverse",
    )(core, held, other)


def coeff_kernel(core, inverse, near, low, snap, keep, send, *, factor):
    cross = near[...] + lax.dot_general(
        low[...], snap[...], FIRST, preferred_element_type=jnp.float32
    )
    value = jnp.dot(inverse[...], cross, precision=HIGHEST) * factor
    chips, sub, _ = keep.shape
    blocks = value.shape[1] // 128
    each = sub // blocks
    first = core[0] == 0
    for q in range(blocks):
        part = value[:, 128 * q : 128 * (q + 1)].reshape(chips, 2 * each, 128)
        one, two = part[:, :each, :], part[:, each:, :]
        keep[:, each * q : each * (q + 1), :] = jnp.where(first, one, two)
        send[:, each * q : each * (q + 1), :] = jnp.where(first, two, one)


def coeff_parts(core, inverse, near, low, snap, factor, chips):
    rank, cols = near.shape
    rows = low.shape[0]
    sub = rank // (2 * chips) * (cols // 128)
    vmem = pl.BlockSpec(memory_space=pltpu.VMEM)
    return pl.pallas_call(
        functools.partial(coeff_kernel, factor=factor),
        in_specs=[pl.BlockSpec(memory_space=pltpu.SMEM)] + [vmem] * 4,
        out_specs=[vmem] * 2,
        out_shape=[jax.ShapeDtypeStruct((chips, sub, 128), jnp.float32)] * 2,
        compiler_params=params(),
        cost_estimate=cost(2 * rows * cols * rank + 12 * rank * rank * cols, 2 * rows * cols),
        name="coeff_parts",
    )(core, inverse, near, low, snap)


def basis_kernel(top, bottom, inverse, out, *, factor, steps):
    dims = (((1,), (1,)), ((), ()))
    mine = jnp.where(pl.program_id(0) < steps, top[...], bottom[...])
    out[...] = lax.dot_general(mine, inverse[...], dims, precision=HIGHEST) * factor


def basis_rows(top, bottom, inverse, factor):
    rows, rank = top.shape
    steps = 2
    tile = rows // steps
    return pl.pallas_call(
        functools.partial(basis_kernel, factor=factor, steps=steps),
        grid=(2 * steps,),
        in_specs=[
            pl.BlockSpec((tile, rank), lambda i: (jnp.minimum(i, steps - 1), 0)),
            pl.BlockSpec((tile, rank), lambda i: (jnp.maximum(i - steps, 0), 0)),
            pl.BlockSpec((rank, rank), lambda i: (0, 0)),
        ],
        out_specs=pl.BlockSpec((tile, rank), lambda i: (i, 0)),
        out_shape=jax.ShapeDtypeStruct((2 * rows, rank), jnp.float32),
        compiler_params=params(),
        cost_estimate=cost(24 * rows * rank * rank, 16 * rows * rank),
        name="basis_rows",
    )(top, bottom, inverse)


def shift(value, axis, by):
    n = lax.axis_size(axis)
    return lax.ppermute(value, axis, [(i, (i + by) % n) for i in range(n)])


def exchange(value, axes):
    return lax.all_to_all(value, axes, 0, 0, tiled=True)


def per_device(snapshots, omega):
    x, c = lax.axis_index("x"), lax.axis_index("c")
    nx, nz, cores = lax.axis_size("x"), lax.axis_size("z"), lax.axis_size("c")
    chips = nz * lax.axis_size("y")
    cols, rank = omega.shape
    rows = snapshots.shape[0] // nx
    half = rows // 2
    total_rows = snapshots.shape[0] * chips * cores
    total_cols = cols * nx
    ahead = lambda d: 2 * lax.rem(x + d, nx)
    at = lambda *places: jnp.stack(places).astype(jnp.int32)
    sketch = functools.partial(sketch_rows, snapshots, omega, half=half)
    half16 = lambda v: v.astype(jnp.float16)

    far = sketch(which=at(lax.rem(x + 2, nx)), per_step=2, scaled=2, pad=PAD, name="far_chunk")
    far_up, far_down = shift(half16(far[0]), "x", 1), shift(half16(far[1]), "x", -1)
    places = at(ahead(1) + 1, ahead(3), ahead(1), ahead(3) + 1)
    near = sketch(which=places, per_step=1, scaled=2, pad=PAD, name="near_chunks")
    near_up, near_down = shift(half16(near[0]), "x", 1), shift(half16(near[1]), "x", -1)
    own = sketch(which=at(x), per_step=2, scaled=0, pad=0, name="own_chunk")
    far_up = shift(relay(far_up, near[2], half), "x", 1)
    far_down = shift(relay(far_down, near[3], half), "x", -1)
    top = own[0] + add_back(near_down, half) + add_back(far_up, half)
    bottom = own[1] + add_back(near_up, half) + add_back(far_down, half)

    tie = lax.optimization_barrier
    block = lambda *ds: at(*[lax.rem(x + d, nx) for d in ds])
    core = c.astype(jnp.int32).reshape(1)
    keep, send, low = gram_of(core, top, bottom)
    held = keep + shift(send, "c", 1)
    left, right = shift(low, "x", 1), shift(low, "x", -1)
    cross = cross_part(snapshots, block(0), [low])
    held, cross = tie((exchange(held.reshape(nz, -1, held.shape[1]), "z"), cross))

    place = lax.rem(x + 2, nx) * rows
    held, cross, place = tie((sum_copies(held, lax.axis_size("y") * nx), cross, place))
    cross = cross_part(snapshots, block(3, 1), [left, right], cross)
    snap = lax.dynamic_slice_in_dim(snapshots, place, rows, 0)
    held, cross, snap = tie((exchange(held, ("y", "x")), cross, snap))

    held, low = tie((sum_copies(held, nz), low))
    across = shift(low, "x", 2)
    held = exchange(held, "z")
    held = held.reshape(-1, held.shape[2])
    other = shift(held, "c", 1)
    inverse = lower_inverse(core, held, other)

    factor = (total_cols / total_rows) ** 0.5
    keep, send = coeff_parts(core, inverse, cross, across, snap, factor, chips)
    both = keep + shift(send, "c", 1)
    coeff = jnp.sum(exchange(both, ("z", "y")), axis=0)
    coeff = coeff.reshape(cols // 128, -1, 128).transpose(1, 0, 2).reshape(-1, cols)

    basis = basis_rows(top, bottom, inverse, total_rows**0.5)
    return basis, coeff


def solution(mesh):
    fine = Mesh(mesh.devices.reshape(8, 4, 2, 4), ("z", "y", "c", "x"))
    space = ("z", "y", "c")
    return jax.shard_map(
        per_device,
        mesh=fine,
        in_specs=(P(space, "x"), P("x", None)),
        out_specs=(P(space + ("x",), None), P(space, "x")),
        check_vma=False,
    )
```

```python
import functools

import jax
import jax.numpy as jnp
from jax import lax
from jax.experimental import pallas as pl
from jax.experimental.pallas import tpu as pltpu
from jax.sharding import Mesh, PartitionSpec as P

HIGHEST = lax.Precision.HIGHEST
PAD = 16
MIB = 1024 * 1024
FIRST = (((0,), (0,)), ((), ()))


def params(mib=16):
    return pltpu.CompilerParams(vmem_limit_bytes=mib * MIB)


def cost(flops, nbytes):
    return pl.CostEstimate(flops=flops, bytes_accessed=nbytes, transcendentals=0)


def sketch_kernel(which, snap, omega, out, *, scaled, pad):
    n, half, _ = out.shape
    half -= pad
    value = jnp.dot(snap[...], omega[...], preferred_element_type=jnp.float32)
    for h in range(n):
        part = value[half * h : half * (h + 1)]
        if pad:
            top = jnp.max(jnp.abs(part), axis=0, keepdims=True)
            power = jnp.ceil(jnp.log2(jnp.maximum(top, 1e-30))) + 1.0
            scale = jnp.exp2(14.0 - power)
            part = part * jnp.where(pl.program_id(0) * n + h < scaled, scale, 1.0)
            out[h, half:, :] = jnp.broadcast_to(power, (pad, power.shape[1]))
        out[h, :half, :] = part


def sketch_rows(snapshots, omega, which, half, per_step, scaled, pad, name):
    cols, rank = omega.shape
    n = which.shape[0]
    return pl.pallas_call(
        functools.partial(sketch_kernel, scaled=scaled, pad=pad),
        grid_spec=pltpu.PrefetchScalarGridSpec(
            num_scalar_prefetch=1,
            grid=(n,),
            in_specs=[
                pl.BlockSpec((per_step * half, cols), lambda i, which: (which[i], 0)),
                pl.BlockSpec((cols, rank), lambda i, which: (0, 0)),
            ],
            out_specs=pl.BlockSpec((per_step, half + pad, rank), lambda i, which: (i, 0, 0)),
        ),
        out_shape=jax.ShapeDtypeStruct((n * per_step, half + pad, rank), jnp.float32),
        compiler_params=params(52),
        cost_estimate=cost(2 * n * per_step * half * cols * rank, 4 * n * per_step * half * cols),
        name=name,
    )(which, snapshots, omega)


def add_back(got, half):
    power = got[half : half + 1].astype(jnp.float32)
    return got[:half].astype(jnp.float32) * jnp.exp2(power - 14.0)


def relay(got, later, half):
    before = got[half : half + 1].astype(jnp.float32)
    power = jnp.maximum(before, later[half : half + 1]) + 1.0
    value = got.astype(jnp.float32) * jnp.exp2(before - 14.0) + later
    value = value * jnp.exp2(14.0 - power)
    row = lax.broadcasted_iota(jnp.int32, value.shape, 0)
    return jnp.where(row < half, value, power).astype(jnp.float16)


def gram_kernel(core, top, bottom, keep, send, low, buf):
    half, rows, rank = top.shape[0], keep.shape[0], top.shape[1]
    gram = lax.dot_general(top[...], top[...], FIRST, precision=HIGHEST) + lax.dot_general(
        bottom[...], bottom[...], FIRST, precision=HIGHEST
    )
    buf[:, :rank] = gram[: rank // 2]
    buf[:, rank:] = gram[rank // 2 :, rank // 2 :]
    keep[...] = buf[pl.ds(pl.multiple_of(core[0] * rows, rows), rows), :]
    send[...] = buf[pl.ds(pl.multiple_of((1 - core[0]) * rows, rows), rows), :]
    low[:half, :] = top[...].astype(low.dtype)
    low[half:, :] = bottom[...].astype(low.dtype)


def gram_of(core, top, bottom):
    rows, rank = top.shape
    vmem = pl.BlockSpec(memory_space=pltpu.VMEM)
    packed = (rank // 2, rank + rank // 2)
    return pl.pallas_call(
        gram_kernel,
        in_specs=[pl.BlockSpec(memory_space=pltpu.SMEM), vmem, vmem],
        out_specs=[vmem] * 3,
        out_shape=[jax.ShapeDtypeStruct((packed[0] // 2, packed[1]), jnp.float32)] * 2
        + [jax.ShapeDtypeStruct((2 * rows, rank), jnp.bfloat16)],
        scratch_shapes=[pltpu.VMEM(packed, jnp.float32)],
        compiler_params=params(),
        cost_estimate=cost(24 * rows * rank * rank, 12 * rows * rank),
        name="gram_of",
    )(core, top, bottom)


def spread_kernel(got, out):
    total = got[0]
    for i in range(1, got.shape[0]):
        total = total + got[i]
    for i in range(out.shape[0]):
        out[i] = total


def sum_copies(got, n):
    return pl.pallas_call(
        spread_kernel,
        out_shape=jax.ShapeDtypeStruct((n,) + got.shape[1:], got.dtype),
        compiler_params=params(),
        name="sum_copies",
    )(got)


def cross_kernel(which, snap, *refs, has_before):
    refs, out = refs[:-1], refs[-1]
    before, lows = (refs[0], refs[1:]) if has_before else (None, refs)
    step = pl.program_id(0)
    for i, low in enumerate(lows):

        @pl.when(step == i)
        def _():
            part = lax.dot_general(low[...], snap[...], FIRST, preferred_element_type=jnp.float32)
            if i:
                out[...] += part
            elif before is not None:
                out[...] = before[...] + part
            else:
                out[...] = part


def cross_part(snapshots, order, lows, before=None):
    rows, rank = lows[0].shape
    cols = snapshots.shape[1]
    n = len(lows)
    whole = lambda i, which: (0, 0)
    start = [] if before is None else [before]
    return pl.pallas_call(
        functools.partial(cross_kernel, has_before=before is not None),
        grid_spec=pltpu.PrefetchScalarGridSpec(
            num_scalar_prefetch=1,
            grid=(n,),
            in_specs=[pl.BlockSpec((rows, cols), lambda i, which: (which[i], 0))]
            + [pl.BlockSpec((rank, cols), whole)] * len(start)
            + [pl.BlockSpec((rows, rank), whole)] * n,
            out_specs=pl.BlockSpec((rank, cols), whole),
        ),
        out_shape=jax.ShapeDtypeStruct((rank, cols), jnp.float32),
        compiler_params=params(52),
        cost_estimate=cost(2 * n * rows * cols * rank, 2 * n * rows * (cols + rank)),
        name="cross_part",
    )(order, snapshots, *start, *lows)


def eliminate(groups, buf):
    shape = groups[0].shape
    sub = lax.broadcasted_iota(jnp.int32, shape, 0)
    lane = lax.broadcasted_iota(jnp.int32, shape, 1)
    spread = lambda v: jnp.broadcast_to(v, shape)
    diags = []
    for g in range(len(groups)):
        k = 8 * g
        cols = {
            i: [spread(groups[i][:, k + j : k + j + 1]) for j in range(8)]
            for i in range(g, len(groups))
        }
        base = g % 2 * 64
        for j in range(8):
            buf[base + 8 * j : base + 8 * j + 8, :] = cols[g][j]
        at = lambda i, j: base + 8 * j + i
        pivot = [[spread(buf[at(i, j) : at(i, j) + 1, :]) for j in range(i + 1)] for i in range(8)]
        inside = (lane >= k) & (lane < k + 8)
        here = jnp.where(inside, jnp.where(lane - k == sub, 1.0, 0.0), groups[g])
        inv, low = [], [[None] * 8 for _ in range(8)]
        for j in range(8):
            if j % 2 == 0:
                a, b, d = pivot[j][j], pivot[j + 1][j], pivot[j + 1][j + 1]
                guess = a * (1.0 / (a * d - b * b))
                inv.append(1.0 / a)
            else:
                inv.append(guess * (2.0 - pivot[j][j] * guess))
            for i in range(j + 1, 8):
                low[i][j] = pivot[i][j] * inv[j]
            for i in range(j + 1, 8):
                for m in range(j + 1, i + 1):
                    pivot[i][m] = pivot[i][m] - low[i][j] * pivot[m][j]
        rows = []
        for i in range(8):
            row = spread(here[i : i + 1, :])
            for j in range(i):
                row = row - low[i][j] * rows[j]
            rows.append(row)
        new, diag = rows[0], pivot[0][0]
        for j in range(1, 8):
            new = jnp.where(sub == j, rows[j], new)
            diag = jnp.where(sub == j, pivot[j][j], diag)
        groups[g] = new
        diags.append(diag)
        for i in range(g + 1, len(groups)):
            mult = []
            for j in range(8):
                c = cols[i][j]
                for q in range(j):
                    c = c - mult[q] * pivot[j][q]
                mult.append(c * inv[j])
            new = jnp.where(inside, 0.0, groups[i])
            for j in range(8):
                new = new - mult[j] * rows[j]
            groups[i] = new
    return [
        jnp.where(lane <= sub + 8 * g, v, 0.0) * lax.rsqrt(d)
        for g, (v, d) in enumerate(zip(groups, diags))
    ]


def block_inverse(block, buf):
    groups = [block[8 * i : 8 * i + 8] for i in range(block.shape[0] // 8)]
    return jnp.concatenate(eliminate(groups, buf), axis=0)


def inverse_kernel(core, held, other, inverse, packed, buf):
    rows, n = held.shape[0], inverse.shape[0] // 2
    packed[pl.ds(pl.multiple_of(core[0] * rows, rows), rows), :] = held[...]
    packed[pl.ds(pl.multiple_of((1 - core[0]) * rows, rows), rows), :] = other[...]
    first = block_inverse(packed[:, :n], buf)
    solved = jnp.dot(first, packed[:, n : 2 * n], precision=HIGHEST)
    inverse[:n, :n] = first
    inverse[:n, n:] = jnp.zeros((n, n), jnp.float32)
    update = lax.dot_general(solved, solved, FIRST, precision=HIGHEST)
    second = block_inverse(packed[:, 2 * n :] - update, buf)
    inverse[n:, n:] = second
    below = lax.dot_general(solved, first, FIRST, precision=HIGHEST)
    inverse[n:, :n] = -jnp.dot(second, below, precision=HIGHEST)


def lower_inverse(core, held, other):
    rows, width = held.shape
    n = width // 3
    vmem = pl.BlockSpec(memory_space=pltpu.VMEM)
    return pl.pallas_call(
        inverse_kernel,
        in_specs=[pl.BlockSpec(memory_space=pltpu.SMEM), vmem, vmem],
        out_specs=vmem,
        out_shape=jax.ShapeDtypeStruct((2 * n, 2 * n), jnp.float32),
        scratch_shapes=[
            pltpu.VMEM((2 * rows, width), jnp.float32),
            pltpu.VMEM((128, n), jnp.float32),
        ],
        compiler_params=params(),
        cost_estimate=cost(5 * 10**9, 4 * rows * width),
        name="lower_inverse",
    )(core, held, other)


def coeff_kernel(core, inverse, near, low, snap, keep, send, *, factor):
    cross = near[...] + lax.dot_general(
        low[...], snap[...], FIRST, preferred_element_type=jnp.float32
    )
    value = jnp.dot(inverse[...], cross, precision=HIGHEST) * factor
    chips, sub, _ = keep.shape
    blocks = value.shape[1] // 128
    each = sub // blocks
    first = core[0] == 0
    for q in range(blocks):
        part = value[:, 128 * q : 128 * (q + 1)].reshape(chips, 2 * each, 128)
        one, two = part[:, :each, :], part[:, each:, :]
        keep[:, each * q : each * (q + 1), :] = jnp.where(first, one, two)
        send[:, each * q : each * (q + 1), :] = jnp.where(first, two, one)


def coeff_parts(core, inverse, near, low, snap, factor, chips):
    rank, cols = near.shape
    rows = low.shape[0]
    sub = rank // (2 * chips) * (cols // 128)
    vmem = pl.BlockSpec(memory_space=pltpu.VMEM)
    return pl.pallas_call(
        functools.partial(coeff_kernel, factor=factor),
        in_specs=[pl.BlockSpec(memory_space=pltpu.SMEM)] + [vmem] * 4,
        out_specs=[vmem] * 2,
        out_shape=[jax.ShapeDtypeStruct((chips, sub, 128), jnp.float32)] * 2,
        compiler_params=params(),
        cost_estimate=cost(2 * rows * cols * rank + 12 * rank * rank * cols, 2 * rows * cols),
        name="coeff_parts",
    )(core, inverse, near, low, snap)


def basis_kernel(top, bottom, inverse, out, *, factor, steps):
    dims = (((1,), (1,)), ((), ()))
    mine = jnp.where(pl.program_id(0) < steps, top[...], bottom[...])
    out[...] = lax.dot_general(mine, inverse[...], dims, precision=HIGHEST) * factor


def basis_rows(top, bottom, inverse, factor):
    rows, rank = top.shape
    steps = 2
    tile = rows // steps
    return pl.pallas_call(
        functools.partial(basis_kernel, factor=factor, steps=steps),
        grid=(2 * steps,),
        in_specs=[
            pl.BlockSpec((tile, rank), lambda i: (jnp.minimum(i, steps - 1), 0)),
            pl.BlockSpec((tile, rank), lambda i: (jnp.maximum(i - steps, 0), 0)),
            pl.BlockSpec((rank, rank), lambda i: (0, 0)),
        ],
        out_specs=pl.BlockSpec((tile, rank), lambda i: (i, 0)),
        out_shape=jax.ShapeDtypeStruct((2 * rows, rank), jnp.float32),
        compiler_params=params(),
        cost_estimate=cost(24 * rows * rank * rank, 16 * rows * rank),
        name="basis_rows",
    )(top, bottom, inverse)


def shift(value, axis, by):
    n = lax.axis_size(axis)
    return lax.ppermute(value, axis, [(i, (i + by) % n) for i in range(n)])


def exchange(value, axes):
    return lax.all_to_all(value, axes, 0, 0, tiled=True)


def per_device(snapshots, omega):
    x, c = lax.axis_index("x"), lax.axis_index("c")
    nx, nz, cores = lax.axis_size("x"), lax.axis_size("z"), lax.axis_size("c")
    chips = nz * lax.axis_size("y")
    cols, rank = omega.shape
    rows = snapshots.shape[0] // nx
    half = rows // 2
    total_rows = snapshots.shape[0] * chips * cores
    total_cols = cols * nx
    ahead = lambda d: 2 * lax.rem(x + d, nx)
    at = lambda *places: jnp.stack(places).astype(jnp.int32)
    sketch = functools.partial(sketch_rows, snapshots, omega, half=half)
    half16 = lambda v: v.astype(jnp.float16)

    far = sketch(which=at(lax.rem(x + 2, nx)), per_step=2, scaled=2, pad=PAD, name="far_chunk")
    far_up, far_down = shift(half16(far[0]), "x", 1), shift(half16(far[1]), "x", -1)
    places = at(ahead(1) + 1, ahead(3))
    near = sketch(which=places, per_step=1, scaled=2, pad=PAD, name="near_halves")
    near_up, near_down = shift(half16(near[0]), "x", 1), shift(half16(near[1]), "x", -1)
    places = at(ahead(1), ahead(3) + 1)
    later = sketch(which=places, per_step=1, scaled=0, pad=PAD, name="relay_halves")
    own = sketch(which=at(x), per_step=2, scaled=0, pad=0, name="own_chunk")
    far_up = shift(relay(far_up, later[0], half), "x", 1)
    far_down = shift(relay(far_down, later[1], half), "x", -1)
    top = own[0] + add_back(near_down, half) + add_back(far_up, half)
    bottom = own[1] + add_back(near_up, half) + add_back(far_down, half)

    tie = lax.optimization_barrier
    block = lambda *ds: at(*[lax.rem(x + d, nx) for d in ds])
    core = c.astype(jnp.int32).reshape(1)
    keep, send, low = gram_of(core, top, bottom)
    held = keep + shift(send, "c", 1)
    left, right = shift(low, "x", 1), shift(low, "x", -1)
    cross = cross_part(snapshots, block(0), [low])
    held, cross = tie((exchange(held.reshape(nz, -1, held.shape[1]), "z"), cross))

    place = lax.rem(x + 2, nx) * rows
    held, cross, place = tie((sum_copies(held, lax.axis_size("y") * nx), cross, place))
    cross = cross_part(snapshots, block(3, 1), [left, right], cross)
    snap = lax.dynamic_slice_in_dim(snapshots, place, rows, 0)
    held, cross, snap = tie((exchange(held, ("y", "x")), cross, snap))

    held, low = tie((sum_copies(held, nz), low))
    across = shift(low, "x", 2)
    held = exchange(held, "z")
    held = held.reshape(-1, held.shape[2])
    other = shift(held, "c", 1)
    inverse = lower_inverse(core, held, other)

    factor = (total_cols / total_rows) ** 0.5
    keep, send = coeff_parts(core, inverse, cross, across, snap, factor, chips)
    both = keep + shift(send, "c", 1)
    coeff = jnp.sum(exchange(both, ("z", "y")), axis=0)
    coeff = coeff.reshape(cols // 128, -1, 128).transpose(1, 0, 2).reshape(-1, cols)

    basis = basis_rows(top, bottom, inverse, total_rows**0.5)
    return basis, coeff


def solution(mesh):
    fine = Mesh(mesh.devices.reshape(8, 4, 2, 4), ("z", "y", "c", "x"))
    space = ("z", "y", "c")
    return jax.shard_map(
        per_device,
        mesh=fine,
        in_specs=(P(space, "x"), P("x", None)),
        out_specs=(P(space + ("x",), None), P(space, "x")),
        check_vma=False,
    )
```
